32 devices in a mesh: seq: 16 (over z, x, core), blk: 2 (over y).
Axes of the slice: x: 2, y: 2, z: 4, core: 2. Of those that a mesh axis runs over, the one named last changes fastest.
Arguments:
- query_states: bfloat16 [4096, 2048], P(('seq', 'blk')), may hold values from -6 to 6
- key_states: bfloat16 [4096, 2048], P(('seq', 'blk')), may hold values from -6 to 6
- value_states: bfloat16 [4096, 2048], P(('seq', 'blk')), may hold values from -6 to 6
- output_grad: bfloat16 [4096, 2048], P(('seq', 'blk')), may hold values from -6 to 6
- near_mask: int32 [32, 2], replicated, may hold values 0 or 1
- motion_count: int32 [32], replicated, may hold values from 0 to 3
Outputs:
- query_grad: bfloat16 [4096, 2048], P(('seq', 'blk'))
- key_grad: bfloat16 [4096, 2048], P(('seq', 'blk'))
- value_grad: bfloat16 [4096, 2048], P(('seq', 'blk'))
The draws below stay inside these ranges and needn't reach their ends.
All inputs are finite; a program needn't handle non-finite values.
Results may differ from the reference program's by a relative error of at most 0.012.
Values may be sent and summed in bfloat16 or wider, within the bound.
A program may use at most 64 MiB of HBM per device.

```python
from functools import partial
import jax
import jax.numpy as jnp
from jax import lax

HEADS = 32
HEAD_DIM = 64
TILE = 128
REACH = 2
TOKENS = 4096
QTILES = 32


def draw_query_states(key, part):
    shape_full = (TOKENS, HEADS * HEAD_DIM)
    result = jnp.clip(jax.random.normal(jax.random.fold_in(key, 1), shape_full, jnp.float32), -4.0, 4.0)
    return result.astype(jnp.bfloat16)


def draw_key_states(key, part):
    shape_full = (TOKENS, HEADS * HEAD_DIM)
    result = jnp.clip(jax.random.normal(jax.random.fold_in(key, 2), shape_full, jnp.float32), -4.0, 4.0)
    return result.astype(jnp.bfloat16)


def place_ends(values, rng, low, largest):
    longest = values.shape.index(max(values.shape))
    spots = []
    for shift in (0, 1):
        where = [jax.random.randint(jax.random.fold_in(rng, axis), (), 0, length) for axis, length in enumerate(values.shape)]
        where[longest] = (where[longest] + shift) % values.shape[longest]
        spots.append(tuple(where))
    return values.at[spots[0]].set(low).at[spots[1]].set(largest)


def levels(key, shape, shards, smallest, high):
    factor_of, own = 1.0, jax.random.fold_in(key, 6)
    for axis_at, shards_of in shards:
        heights = jnp.exp(jax.random.uniform(jax.random.fold_in(own, axis_at), (shards_of,), jnp.float32, smallest / len(shards), high / len(shards)))
        factor_of = factor_of * jnp.repeat(heights, shape[axis_at] // shards_of).reshape([-1 if axis == axis_at else 1 for axis in range(len(shape))])
    return factor_of


def gaussian(key, dims, scale, most, shards=(), kind=jnp.bfloat16):
    entries = scale * jax.random.normal(key, dims, jnp.float32)
    if shards:
        entries = entries * levels(key, dims, shards, -0.22, 0.18)
    return jnp.clip(entries, -most, most).astype(kind)


def setup_inputs(seed: int = 0) -> dict:
    splits = jax.random.split(jax.random.key(seed), 7)
    return {
        "query_states": draw_query_states(jax.random.fold_in(splits[6], 71), 0),
        "key_states": draw_key_states(jax.random.fold_in(splits[6], 71), 0),
        "value_states": gaussian(splits[2], (TOKENS, HEADS * HEAD_DIM), 1.0, 6.0, ((0, 32),)),
        "output_grad": gaussian(splits[3], (TOKENS, HEADS * HEAD_DIM), 1.0, 6.0, ((0, 32),)),
        "near_mask": place_ends((jax.random.randint(splits[4], (QTILES, 2), 0, 4) < 3).astype(jnp.int32), jax.random.fold_in(splits[4], 1), 0, 1),
        "motion_count": place_ends(jax.random.randint(splits[5], (QTILES,), 0, 4), jax.random.fold_in(splits[5], 1), 0, 3).astype(jnp.int32),
    }


def tile_allow(mask_rows, motion_rows, query_tile0, key_tile0, tiles_all, query_tiles, key_tiles, tile_size):
    query_ids = query_tile0 + jnp.arange(query_tiles, dtype=jnp.int32)[:, None]
    key_ids = key_tile0 + jnp.arange(key_tiles, dtype=jnp.int32)[None, :]
    spread = key_ids - query_ids
    near = (spread == 0) | (spread == -1) & (mask_rows[:, 0:1] == 1) | (spread == 1) & (mask_rows[:, 1:2] == 1)
    far_ok = (jnp.abs(spread) >= 2) & (jnp.abs(spread) <= REACH) & (motion_rows[:, None] >= 2)
    inside = (key_ids >= 0) & (key_ids < tiles_all)
    tile_ok = (near | far_ok) & inside
    spread_out = jnp.broadcast_to(tile_ok[:, None, :, None], (query_tiles, tile_size, key_tiles, tile_size))
    return spread_out.reshape(query_tiles * tile_size, key_tiles * tile_size)

def block_grad(query_rows, key_rows, value_rows, grad_rows, allowed, scale_factor):
    query_wide = query_rows.astype(jnp.float32)
    key_wide = key_rows.astype(jnp.float32)
    value_wide = value_rows.astype(jnp.float32)
    grad_wide = grad_rows.astype(jnp.float32)
    scores = jnp.dot(query_wide, key_wide.T, preferred_element_type=jnp.float32) * scale_factor
    scores = jnp.where(allowed, scores, -1e+30)
    row_max = lax.optimization_barrier(jnp.max(scores, axis=1, keepdims=True))
    weights_raw = jnp.exp(scores - row_max)
    probs = weights_raw / lax.optimization_barrier(jnp.sum(weights_raw, axis=1, keepdims=True))
    probs_b = probs.astype(jnp.bfloat16)
    probs_wide = probs_b.astype(jnp.float32)
    attn_out = jnp.dot(probs_wide, value_wide, preferred_element_type=jnp.float32)
    delta = lax.optimization_barrier(jnp.sum(grad_wide * attn_out, axis=1, keepdims=True))
    dprobs = jnp.dot(grad_wide, value_wide.T, preferred_element_type=jnp.float32)
    dscores = (probs * (dprobs - delta)).astype(jnp.bfloat16)
    dscores_wide = dscores.astype(jnp.float32)
    query_part = jnp.dot(dscores_wide, key_wide, preferred_element_type=jnp.float32) * scale_factor
    key_part = jnp.dot(dscores_wide.T, query_wide, preferred_element_type=jnp.float32) * scale_factor
    value_part = jnp.dot(probs_wide.T, grad_wide, preferred_element_type=jnp.float32)
    return (query_part, key_part, value_part)

def reference(query_states, key_states, value_states, output_grad, near_mask, motion_count):
    span = REACH * TILE
    blocks = TOKENS // span
    scale_factor = float(HEAD_DIM) ** (-0.5)
    queries = query_states.reshape(TOKENS, HEADS, HEAD_DIM)
    grads_in = output_grad.reshape(TOKENS, HEADS, HEAD_DIM)
    padding = ((span, span), (0, 0), (0, 0))
    keys_pad = jnp.pad(key_states.reshape(TOKENS, HEADS, HEAD_DIM), padding)
    values_pad = jnp.pad(value_states.reshape(TOKENS, HEADS, HEAD_DIM), padding)
    per_head = jax.vmap(partial(block_grad, scale_factor=scale_factor), in_axes=(1, 1, 1, 1, None), out_axes=1)
    zeros_block = jnp.zeros((2, span, HEADS, HEAD_DIM), jnp.float32)

    def step_block(running, block_index):
        pending_prev, pending_now = running
        row_start = block_index * span
        query_rows = lax.dynamic_slice_in_dim(queries, row_start, span, 0)
        grad_rows = lax.dynamic_slice_in_dim(grads_in, row_start, span, 0)
        key_rows = lax.dynamic_slice_in_dim(keys_pad, row_start, 3 * span, 0)
        value_rows = lax.dynamic_slice_in_dim(values_pad, row_start, 3 * span, 0)
        query_tile0 = (row_start // TILE).astype(jnp.int32)
        mask_rows = lax.dynamic_slice_in_dim(near_mask, query_tile0, span // TILE, 0)
        motion_rows = lax.dynamic_slice_in_dim(motion_count, query_tile0, span // TILE, 0)
        allowed = tile_allow(mask_rows, motion_rows, query_tile0, query_tile0 - REACH, QTILES, span // TILE, 3 * span // TILE, TILE)
        query_part, key_part, value_part = per_head(query_rows, key_rows, value_rows, grad_rows, allowed)
        both = jnp.stack([key_part, value_part])
        finished = pending_prev + both[:, 0:span]
        new_prev = pending_now + both[:, span:2 * span]
        new_now = both[:, 2 * span:3 * span]
        return ((new_prev, new_now), (query_part.astype(jnp.bfloat16), finished.astype(jnp.bfloat16)))
    indices = jnp.arange(blocks, dtype=jnp.int32)
    (last_prev, last_now), (query_blocks, done_blocks) = lax.scan(step_block, (zeros_block, zeros_block), indices)
    query_grad = query_blocks.reshape(TOKENS, HEADS * HEAD_DIM)
    tail = last_prev.astype(jnp.bfloat16)[None]
    kv_blocks = jnp.concatenate([done_blocks[1:], tail], axis=0)
    key_grad = kv_blocks[:, 0].reshape(TOKENS, HEADS * HEAD_DIM)
    value_grad = kv_blocks[:, 1].reshape(TOKENS, HEADS * HEAD_DIM)
    return (query_grad, key_grad, value_grad)
```

```python
import functools

import jax
import jax.numpy as jnp
from jax import lax
from jax.experimental import pallas as pl
from jax.experimental.pallas import tpu as pltpu
from jax.sharding import PartitionSpec as P

HEAD_DIM = 64
TILE = 128
REACH = 2
RIM = REACH * TILE
WINDOW = 2 * REACH + 1
PAIR = 2 * HEAD_DIM
WIDTH = 128
FINISH_LAG = 2
NEG = -1e30
MESH = pl.DeviceIdType.MESH
F32 = jnp.float32
BF16 = jnp.bfloat16


def stack_heads(rows, scale):
    lane = lax.broadcasted_iota(jnp.int32, rows.shape, 1)
    zero = jnp.zeros_like(rows)
    rows = rows * jnp.asarray(scale, rows.dtype)
    return jnp.concatenate(
        [jnp.where(lane < HEAD_DIM, rows, zero), jnp.where(lane >= HEAD_DIM, rows, zero)], axis=0
    )


def unit_grad(query, grad, keys, values, allow):
    contract_last = (((1,), (1,)), ((), ()))
    contract_first = (((0,), (0,)), ((), ()))
    scale = float(HEAD_DIM) ** (-0.5)
    query_two = stack_heads(query, scale)
    grad_two = stack_heads(grad, 1.0)
    scores = lax.dot_general(keys, query_two, contract_last, preferred_element_type=F32)
    dprobs = lax.dot_general(values, grad_two, contract_last, preferred_element_type=F32)
    tiles = [scores[j * TILE : (j + 1) * TILE] for j in range(WINDOW)]
    peak = None
    for ok, tile in zip(allow, tiles):
        top = jnp.where(ok, jnp.max(tile, axis=0, keepdims=True), NEG)
        peak = top if peak is None else jnp.maximum(peak, top)
    raw = [jnp.exp(tile - jnp.where(ok, peak, -NEG)) for ok, tile in zip(allow, tiles)]
    raw = jnp.concatenate(raw, axis=0)
    probs = raw * (1.0 / jnp.sum(raw, axis=0, keepdims=True))
    delta = jnp.sum(probs * dprobs, axis=0, keepdims=True)
    dscores = (probs * (dprobs - delta)).astype(BF16)
    value_part = jnp.dot(probs.astype(BF16), grad_two, preferred_element_type=F32)
    key_part = jnp.dot(dscores, query_two, preferred_element_type=F32)
    both = lax.dot_general(keys, dscores, contract_first, preferred_element_type=F32)
    row = lax.broadcasted_iota(jnp.int32, (PAIR, TILE), 0)
    query_part = jnp.where(row < HEAD_DIM, both[:, :TILE], both[:, TILE:])
    return (query_part.T * scale).astype(BF16), key_part, value_part


def kernel(
    seqs, group, feats,
    q_in, k_in, v_in, g_in, near, motion,
    dq_out, dk_out, dv_out,
    qg, kv, dq, acc, part_out, part_in, done,
    in_send, in_recv, halo_send, halo_recv, part_send, part_recv, out_send, out_recv,
):
    seq, blk = lax.axis_index("seq"), lax.axis_index("blk")
    chunks = feats // WIDTH
    own = group * TILE
    has_left, has_right = seq > 0, seq < seqs - 1
    left, right = (seq - 1, blk), (seq + 1, blk)
    tiles_all = near.shape[0]
    inputs = (k_in, v_in, q_in, g_in)
    outputs = (dq_out, dk_out, dv_out)

    barrier = pltpu.get_barrier_semaphore()
    for r in range(1, group):
        pl.semaphore_signal(barrier, inc=1, device_id=(seq, lax.rem(blk + r, group)), device_id_type=MESH)

    @pl.when(has_left)
    def _():
        pl.semaphore_signal(barrier, inc=1, device_id=left, device_id_type=MESH)

    @pl.when(has_right)
    def _():
        pl.semaphore_signal(barrier, inc=1, device_id=right, device_id_type=MESH)

    pl.semaphore_wait(barrier, group - 1 + has_left.astype(jnp.int32) + has_right.astype(jnp.int32))

    def columns(owner, c):
        return pl.ds(pl.multiple_of(owner * feats + c * WIDTH, 128), WIDTH)

    def tile_rows(tile, first=0):
        return pl.ds(pl.multiple_of(first + tile * TILE, TILE), TILE)

    def in_place(a, c, tile):
        if a < 2:
            return kv.at[c, a, tile_rows(tile, RIM)]
        return qg.at[c, a - 2, tile_rows(tile)]

    def in_local(a, c):
        return pltpu.make_async_copy(inputs[a].at[:, columns(blk, c)], in_place(a, c, blk), in_recv.at[c, a, 0])

    def in_remote(a, c, r):
        peer = lax.rem(blk + r, group)
        return pltpu.make_async_remote_copy(
            src_ref=inputs[a].at[:, columns(peer, c)],
            dst_ref=in_place(a, c, blk),
            send_sem=in_send.at[c, a, r - 1],
            recv_sem=in_recv.at[c, a, r],
            device_id=(seq, peer),
            device_id_type=MESH,
        )

    def halo(c, side):
        source = RIM if side == 0 else own
        target = RIM + own if side == 0 else 0
        return pltpu.make_async_remote_copy(
            src_ref=kv.at[c, :, pl.ds(source, RIM)],
            dst_ref=kv.at[c, :, pl.ds(target, RIM)],
            send_sem=halo_send.at[c, side],
            recv_sem=halo_recv.at[c, side],
            device_id=left if side == 0 else right,
            device_id_type=MESH,
        )

    def partial(c, side):
        return pltpu.make_async_remote_copy(
            src_ref=part_out.at[c, side],
            dst_ref=part_in.at[c, side],
            send_sem=part_send.at[c, side],
            recv_sem=part_recv.at[c, side],
            device_id=left if side == 0 else right,
            device_id_type=MESH,
        )

    def out_source(a, c, tile):
        if a == 0:
            return dq.at[c, tile_rows(tile)]
        return done.at[c, a - 1, tile_rows(tile)]

    def out_local(a, c):
        return pltpu.make_async_copy(
            out_source(a, c, blk), outputs[a].at[:, columns(blk, c)], out_recv.at[c, a, 0]
        )

    def out_remote(a, c, r):
        peer = lax.rem(blk + r, group)
        return pltpu.make_async_remote_copy(
            src_ref=out_source(a, c, peer),
            dst_ref=outputs[a].at[:, columns(blk, c)],
            send_sem=out_send.at[c, a, r - 1],
            recv_sem=out_recv.at[c, a, r],
            device_id=(seq, peer),
            device_id_type=MESH,
        )

    def sides(action):
        pl.when(has_left)(lambda: action(0))
        pl.when(has_right)(lambda: action(1))

    def arrivals(action):
        pl.when(has_right)(lambda: action(0))
        pl.when(has_left)(lambda: action(1))

    def send_in(c, _):
        for a in range(4):
            for r in range(1, group):
                in_remote(a, c, r).start()
            in_local(a, c).start()
        return 0

    lax.fori_loop(0, chunks, send_in, 0)

    @pl.when(jnp.logical_not(has_left))
    def _():
        kv[:, :, 0:RIM, :] = jnp.zeros((chunks, 2, RIM, WIDTH), BF16)
        part_in[:, 1] = jnp.zeros((chunks, 2, RIM, WIDTH), BF16)

    @pl.when(jnp.logical_not(has_right))
    def _():
        kv[:, :, RIM + own :, :] = jnp.zeros((chunks, 2, RIM, WIDTH), BF16)
        part_in[:, 0] = jnp.zeros((chunks, 2, RIM, WIDTH), BF16)

    allow = []
    for tile in range(group):
        at = seq * group + tile
        far = motion[at] >= 2
        oks = [far & (at >= 2), (near[at, 0] == 1) & (at >= 1), None,
               (near[at, 1] == 1) & (at + 1 < tiles_all), far & (at + 2 < tiles_all)]
        oks[2] = at >= 0
        allow.append(oks)

    def wait_in(c, arrays):
        for a in arrays:
            in_local(a, c).wait()
            for r in range(1, group):
                in_remote(a, c, r).wait_recv()

    def send_halo(c):
        wait_in(c, (0, 1))
        sides(lambda side: halo(c, side).start())

    def compute(c):
        wait_in(c, (2, 3))
        arrivals(lambda side: halo(c, side).wait_recv())
        for p in range(WIDTH // PAIR):
            cols = slice(p * PAIR, (p + 1) * PAIR)
            for tile in range(group):
                rows = slice(tile * TILE, (tile + 1) * TILE)
                span = slice(tile * TILE, (tile + WINDOW) * TILE)
                query_part, key_part, value_part = unit_grad(
                    qg[c, 0, rows, cols], qg[c, 1, rows, cols], kv[c, 0, span, cols], kv[c, 1, span, cols],
                    allow[tile],
                )
                dq[c, rows, cols] = query_part
                for a, part in ((0, key_part), (1, value_part)):
                    if tile == 0:
                        acc[c, a, span, cols] = part
                    else:
                        old = slice(tile * TILE, (tile + WINDOW - 1) * TILE)
                        new = slice((tile + WINDOW - 1) * TILE, (tile + WINDOW) * TILE)
                        acc[c, a, old, cols] = acc[c, a, old, cols] + part[: (WINDOW - 1) * TILE]
                        acc[c, a, new, cols] = part[(WINDOW - 1) * TILE :]
        part_out[c, 0] = acc[c, :, 0:RIM].astype(BF16)
        part_out[c, 1] = acc[c, :, RIM + own :].astype(BF16)
        sides(lambda side: partial(c, side).start())
        send_out(c, (0,))

    def send_out(c, arrays):
        for a in arrays:
            for r in range(1, group):
                out_remote(a, c, r).start()
            out_local(a, c).start()

    def finish(c):
        arrivals(lambda side: partial(c, side).wait_recv())
        total = acc[c, :, RIM : RIM + own]
        first = part_in[c, 1].astype(F32)
        last = part_in[c, 0].astype(F32)
        if group == REACH:
            done[c] = (total + first + last).astype(BF16)
        else:
            done[c, :, 0 : own - RIM] = total[:, 0 : own - RIM].astype(BF16)
            done[c, :, 0:RIM] = (total[:, 0:RIM] + first).astype(BF16)
            tail = total[:, own - RIM :] + last
            if own < 2 * RIM:
                tail = tail + jnp.pad(first, ((0, 0), (0, own - RIM), (0, 0)))[:, own - RIM :]
            done[c, :, own - RIM :] = tail.astype(BF16)
        send_out(c, (1, 2))

    send_halo(0)
    if chunks > 1:
        send_halo(1)

    def step(c, _):
        pl.when(c + 2 < chunks)(lambda: send_halo(c + 2))
        compute(c)
        pl.when(c >= FINISH_LAG)(lambda: finish(c - FINISH_LAG))
        return 0

    lax.fori_loop(0, chunks, step, 0)
    lax.fori_loop(max(chunks - FINISH_LAG, 0), chunks, lambda c, _: (finish(c), 0)[1], 0)

    def drain(c, _):
        for a in range(4):
            for r in range(1, group):
                in_remote(a, c, r).wait_send()
        sides(lambda side: halo(c, side).wait_send())
        sides(lambda side: partial(c, side).wait_send())
        for a in range(3):
            out_local(a, c).wait()
            for r in range(1, group):
                out_remote(a, c, r).wait_send()
                out_remote(a, c, r).wait_recv()
        return 0

    lax.fori_loop(0, chunks, drain, 0)


def per_device(seqs, group, query_states, key_states, value_states, output_grad, near_mask, motion_count):
    rows, width = query_states.shape
    assert rows == TILE
    feats = width // group
    chunks = feats // WIDTH
    own = group * TILE
    window = own + 2 * RIM
    result = jax.ShapeDtypeStruct((rows, width), BF16)
    dma = pltpu.SemaphoreType.DMA
    return pl.pallas_call(
        functools.partial(kernel, seqs, group, feats),
        out_shape=(result, result, result),
        in_specs=[pl.BlockSpec(memory_space=pl.ANY)] * 4 + [pl.BlockSpec(memory_space=pltpu.SMEM)] * 2,
        out_specs=[pl.BlockSpec(memory_space=pl.ANY)] * 3,
        scratch_shapes=[
            pltpu.VMEM((chunks, 2, own, WIDTH), BF16),
            pltpu.VMEM((chunks, 2, window, WIDTH), BF16),
            pltpu.VMEM((chunks, own, WIDTH), BF16),
            pltpu.VMEM((chunks, 2, window, WIDTH), F32),
            pltpu.VMEM((chunks, 2, 2, RIM, WIDTH), BF16),
            pltpu.VMEM((chunks, 2, 2, RIM, WIDTH), BF16),
            pltpu.VMEM((chunks, 2, own, WIDTH), BF16),
            dma((chunks, 4, group - 1)),
            dma((chunks, 4, group)),
            dma((chunks, 2)),
            dma((chunks, 2)),
            dma((chunks, 2)),
            dma((chunks, 2)),
            dma((chunks, 3, group - 1)),
            dma((chunks, 3, group)),
        ],
        compiler_params=pltpu.CompilerParams(
            collective_id=0, has_side_effects=True, vmem_limit_bytes=48 * 1024 * 1024
        ),
    )(query_states, key_states, value_states, output_grad, near_mask, motion_count)


def solution(mesh):
    tokens = P(("seq", "blk"), None)
    return jax.shard_map(
        functools.partial(per_device, mesh.shape["seq"], mesh.shape["blk"]),
        mesh=mesh,
        in_specs=(tokens, tokens, tokens, tokens, P(), P()),
        out_specs=(tokens, tokens, tokens),
        check_vma=False,
    )
```

```python
import functools

import jax
import jax.numpy as jnp
from jax import lax
from jax.experimental import pallas as pl
from jax.experimental.pallas import tpu as pltpu
from jax.sharding import PartitionSpec as P

HEAD_DIM = 64
TILE = 128
REACH = 2
RIM = REACH * TILE
WINDOW = 2 * REACH + 1
PAIR = 2 * HEAD_DIM
WIDTH = 256
FINISH_LAG = 2
NEG = -1e30
MESH = pl.DeviceIdType.MESH
F32 = jnp.float32
BF16 = jnp.bfloat16


def stack_heads(rows, scale):
    lane = lax.broadcasted_iota(jnp.int32, rows.shape, 1)
    zero = jnp.zeros_like(rows)
    rows = rows * jnp.asarray(scale, rows.dtype)
    return jnp.concatenate(
        [jnp.where(lane < HEAD_DIM, rows, zero), jnp.where(lane >= HEAD_DIM, rows, zero)], axis=0
    )


def unit_grad(query, grad, keys, values, allow):
    contract_last = (((1,), (1,)), ((), ()))
    contract_first = (((0,), (0,)), ((), ()))
    scale = float(HEAD_DIM) ** (-0.5)
    query_two = stack_heads(query, scale)
    grad_two = stack_heads(grad, 1.0)
    scores = lax.dot_general(keys, query_two, contract_last, preferred_element_type=F32)
    dprobs = lax.dot_general(values, grad_two, contract_last, preferred_element_type=F32)
    tiles = [scores[j * TILE : (j + 1) * TILE] for j in range(WINDOW)]
    peak = None
    for ok, tile in zip(allow, tiles):
        top = jnp.where(ok, jnp.max(tile, axis=0, keepdims=True), NEG)
        peak = top if peak is None else jnp.maximum(peak, top)
    raw = [jnp.exp(tile - jnp.where(ok, peak, -NEG)) for ok, tile in zip(allow, tiles)]
    raw = jnp.concatenate(raw, axis=0)
    probs = raw * (1.0 / jnp.sum(raw, axis=0, keepdims=True))
    delta = jnp.sum(probs * dprobs, axis=0, keepdims=True)
    dscores = (probs * (dprobs - delta)).astype(BF16)
    value_part = jnp.dot(probs.astype(BF16), grad_two, preferred_element_type=F32)
    key_part = jnp.dot(dscores, query_two, preferred_element_type=F32)
    both = lax.dot_general(keys, dscores, contract_first, preferred_element_type=F32)
    row = lax.broadcasted_iota(jnp.int32, (PAIR, TILE), 0)
    query_part = jnp.where(row < HEAD_DIM, both[:, :TILE], both[:, TILE:])
    return (query_part.T * scale).astype(BF16), key_part, value_part


def kernel(
    seqs, group, feats,
    q_in, k_in, v_in, g_in, near, motion,
    dq_out, dk_out, dv_out,
    qg, kv, dq, acc, part_out, part_in, done,
    in_send, in_recv, halo_send, halo_recv, part_send, part_recv, out_send, out_recv,
):
    seq, blk = lax.axis_index("seq"), lax.axis_index("blk")
    chunks = feats // WIDTH
    own = group * TILE
    has_left, has_right = seq > 0, seq < seqs - 1
    left, right = (seq - 1, blk), (seq + 1, blk)
    tiles_all = near.shape[0]
    inputs = (k_in, v_in, q_in, g_in)
    outputs = (dq_out, dk_out, dv_out)

    barrier = pltpu.get_barrier_semaphore()
    for r in range(1, group):
        pl.semaphore_signal(barrier, inc=1, device_id=(seq, lax.rem(blk + r, group)), device_id_type=MESH)

    @pl.when(has_left)
    def _():
        pl.semaphore_signal(barrier, inc=1, device_id=left, device_id_type=MESH)

    @pl.when(has_right)
    def _():
        pl.semaphore_signal(barrier, inc=1, device_id=right, device_id_type=MESH)

    pl.semaphore_wait(barrier, group - 1 + has_left.astype(jnp.int32) + has_right.astype(jnp.int32))

    def columns(owner, c):
        return pl.ds(pl.multiple_of(owner * feats + c * WIDTH, 128), WIDTH)

    def tile_rows(tile, first=0):
        return pl.ds(pl.multiple_of(first + tile * TILE, TILE), TILE)

    def in_place(a, c, tile):
        if a < 2:
            return kv.at[c, a, tile_rows(tile, RIM)]
        return qg.at[c, a - 2, tile_rows(tile)]

    def in_local(a, c):
        return pltpu.make_async_copy(inputs[a].at[:, columns(blk, c)], in_place(a, c, blk), in_recv.at[c, a, 0])

    def in_remote(a, c, r):
        peer = lax.rem(blk + r, group)
        return pltpu.make_async_remote_copy(
            src_ref=inputs[a].at[:, columns(peer, c)],
            dst_ref=in_place(a, c, blk),
            send_sem=in_send.at[c, a, r - 1],
            recv_sem=in_recv.at[c, a, r],
            device_id=(seq, peer),
            device_id_type=MESH,
        )

    def halo(c, side):
        source = RIM if side == 0 else own
        target = RIM + own if side == 0 else 0
        return pltpu.make_async_remote_copy(
            src_ref=kv.at[c, :, pl.ds(source, RIM)],
            dst_ref=kv.at[c, :, pl.ds(target, RIM)],
            send_sem=halo_send.at[c, side],
            recv_sem=halo_recv.at[c, side],
            device_id=left if side == 0 else right,
            device_id_type=MESH,
        )

    def partial(c, side):
        return pltpu.make_async_remote_copy(
            src_ref=part_out.at[c, side],
            dst_ref=part_in.at[c, side],
            send_sem=part_send.at[c, side],
            recv_sem=part_recv.at[c, side],
            device_id=left if side == 0 else right,
            device_id_type=MESH,
        )

    def out_source(a, c, tile):
        if a == 0:
            return dq.at[c, tile_rows(tile)]
        return done.at[c, a - 1, tile_rows(tile)]

    def out_local(a, c):
        return pltpu.make_async_copy(
            out_source(a, c, blk), outputs[a].at[:, columns(blk, c)], out_recv.at[c, a, 0]
        )

    def out_remote(a, c, r):
        peer = lax.rem(blk + r, group)
        return pltpu.make_async_remote_copy(
            src_ref=out_source(a, c, peer),
            dst_ref=outputs[a].at[:, columns(blk, c)],
            send_sem=out_send.at[c, a, r - 1],
            recv_sem=out_recv.at[c, a, r],
            device_id=(seq, peer),
            device_id_type=MESH,
        )

    def sides(action):
        pl.when(has_left)(lambda: action(0))
        pl.when(has_right)(lambda: action(1))

    def arrivals(action):
        pl.when(has_right)(lambda: action(0))
        pl.when(has_left)(lambda: action(1))

    def send_in(c, _):
        for a in range(4):
            for r in range(1, group):
                in_remote(a, c, r).start()
            in_local(a, c).start()
        return 0

    lax.fori_loop(0, chunks, send_in, 0)

    @pl.when(jnp.logical_not(has_left))
    def _():
        kv[:, :, 0:RIM, :] = jnp.zeros((chunks, 2, RIM, WIDTH), BF16)
        part_in[:, 1] = jnp.zeros((chunks, 2, RIM, WIDTH), BF16)

    @pl.when(jnp.logical_not(has_right))
    def _():
        kv[:, :, RIM + own :, :] = jnp.zeros((chunks, 2, RIM, WIDTH), BF16)
        part_in[:, 0] = jnp.zeros((chunks, 2, RIM, WIDTH), BF16)

    allow = []
    for tile in range(group):
        at = seq * group + tile
        far = motion[at] >= 2
        oks = [far & (at >= 2), (near[at, 0] == 1) & (at >= 1), None,
               (near[at, 1] == 1) & (at + 1 < tiles_all), far & (at + 2 < tiles_all)]
        oks[2] = at >= 0
        allow.append(oks)

    def wait_in(c, arrays):
        for a in arrays:
            in_local(a, c).wait()
            for r in range(1, group):
                in_remote(a, c, r).wait_recv()

    def send_halo(c):
        wait_in(c, (0, 1))
        sides(lambda side: halo(c, side).start())

    def compute(c):
        wait_in(c, (2, 3))
        arrivals(lambda side: halo(c, side).wait_recv())
        for p in range(WIDTH // PAIR):
            cols = slice(p * PAIR, (p + 1) * PAIR)
            for tile in range(group):
                rows = slice(tile * TILE, (tile + 1) * TILE)
                span = slice(tile * TILE, (tile + WINDOW) * TILE)
                query_part, key_part, value_part = unit_grad(
                    qg[c, 0, rows, cols], qg[c, 1, rows, cols], kv[c, 0, span, cols], kv[c, 1, span, cols],
                    allow[tile],
                )
                dq[c, rows, cols] = query_part
                for a, part in ((0, key_part), (1, value_part)):
                    if tile == 0:
                        acc[c, a, span, cols] = part
                    else:
                        old = slice(tile * TILE, (tile + WINDOW - 1) * TILE)
                        new = slice((tile + WINDOW - 1) * TILE, (tile + WINDOW) * TILE)
                        acc[c, a, old, cols] = acc[c, a, old, cols] + part[: (WINDOW - 1) * TILE]
                        acc[c, a, new, cols] = part[(WINDOW - 1) * TILE :]
        part_out[c, 0] = acc[c, :, 0:RIM].astype(BF16)
        part_out[c, 1] = acc[c, :, RIM + own :].astype(BF16)
        sides(lambda side: partial(c, side).start())
        send_out(c, (0,))

    def send_out(c, arrays):
        for a in arrays:
            for r in range(1, group):
                out_remote(a, c, r).start()
            out_local(a, c).start()

    def finish(c):
        arrivals(lambda side: partial(c, side).wait_recv())
        total = acc[c, :, RIM : RIM + own]
        first = part_in[c, 1].astype(F32)
        last = part_in[c, 0].astype(F32)
        if group == REACH:
            done[c] = (total + first + last).astype(BF16)
        else:
            done[c, :, 0 : own - RIM] = total[:, 0 : own - RIM].astype(BF16)
            done[c, :, 0:RIM] = (total[:, 0:RIM] + first).astype(BF16)
            tail = total[:, own - RIM :] + last
            if own < 2 * RIM:
                tail = tail + jnp.pad(first, ((0, 0), (0, own - RIM), (0, 0)))[:, own - RIM :]
            done[c, :, own - RIM :] = tail.astype(BF16)
        send_out(c, (1, 2))

    send_halo(0)
    if chunks > 1:
        send_halo(1)

    def step(c, _):
        pl.when(c + 2 < chunks)(lambda: send_halo(c + 2))
        compute(c)
        pl.when(c >= FINISH_LAG)(lambda: finish(c - FINISH_LAG))
        return 0

    lax.fori_loop(0, chunks, step, 0)
    lax.fori_loop(max(chunks - FINISH_LAG, 0), chunks, lambda c, _: (finish(c), 0)[1], 0)

    def drain(c, _):
        for a in range(4):
            for r in range(1, group):
                in_remote(a, c, r).wait_send()
        sides(lambda side: halo(c, side).wait_send())
        sides(lambda side: partial(c, side).wait_send())
        for a in range(3):
            out_local(a, c).wait()
            for r in range(1, group):
                out_remote(a, c, r).wait_send()
                out_remote(a, c, r).wait_recv()
        return 0

    lax.fori_loop(0, chunks, drain, 0)


def per_device(seqs, group, query_states, key_states, value_states, output_grad, near_mask, motion_count):
    rows, width = query_states.shape
    assert rows == TILE
    feats = width // group
    chunks = feats // WIDTH
    own = group * TILE
    window = own + 2 * RIM
    result = jax.ShapeDtypeStruct((rows, width), BF16)
    dma = pltpu.SemaphoreType.DMA
    return pl.pallas_call(
        functools.partial(kernel, seqs, group, feats),
        out_shape=(result, result, result),
        in_specs=[pl.BlockSpec(memory_space=pl.ANY)] * 4 + [pl.BlockSpec(memory_space=pltpu.SMEM)] * 2,
        out_specs=[pl.BlockSpec(memory_space=pl.ANY)] * 3,
        scratch_shapes=[
            pltpu.VMEM((chunks, 2, own, WIDTH), BF16),
            pltpu.VMEM((chunks, 2, window, WIDTH), BF16),
            pltpu.VMEM((chunks, own, WIDTH), BF16),
            pltpu.VMEM((chunks, 2, window, WIDTH), F32),
            pltpu.VMEM((chunks, 2, 2, RIM, WIDTH), BF16),
            pltpu.VMEM((chunks, 2, 2, RIM, WIDTH), BF16),
            pltpu.VMEM((chunks, 2, own, WIDTH), BF16),
            dma((chunks, 4, group - 1)),
            dma((chunks, 4, group)),
            dma((chunks, 2)),
            dma((chunks, 2)),
            dma((chunks, 2)),
            dma((chunks, 2)),
            dma((chunks, 3, group - 1)),
            dma((chunks, 3, group)),
        ],
        compiler_params=pltpu.CompilerParams(
            collective_id=0, has_side_effects=True, vmem_limit_bytes=48 * 1024 * 1024
        ),
    )(query_states, key_states, value_states, output_grad, near_mask, motion_count)


def solution(mesh):
    tokens = P(("seq", "blk"), None)
    return jax.shard_map(
        functools.partial(per_device, mesh.shape["seq"], mesh.shape["blk"]),
        mesh=mesh,
        in_specs=(tokens, tokens, tokens, tokens, P(), P()),
        out_specs=(tokens, tokens, tokens),
        check_vma=False,
    )
```
